32 devices in a mesh: grp: 2 (over x), elem: 8 (over z, y), lev: 2 (over core).
Axes of the slice: x: 2, y: 2, z: 4, core: 2. Of those that a mesh axis runs over, the one named last changes fastest.
Arguments:
- tracer_field: float32 [2, 48, 16, 4096], P(None, 'lev', None, ('grp', 'elem')), parts along dimension 3, may hold values from -6 to 6
- velocity: float32 [2, 48, 16, 4096], P(None, 'lev', None, ('grp', 'elem')), parts along dimension 3, may hold values from -3 to 3
- node_mass: float32 [16, 4096], P(None, ('grp', 'elem')), parts along dimension 1, may hold values from 0.5 to 2
- neighbours: int32 [4, 4096], P(None, ('grp', 'elem')), parts along dimension 1, may hold values from 0 to 2047, as said below
- seam_flips: int32 [4, 4096], P(None, ('grp', 'elem')), parts along dimension 1, may hold values from 0 to 1, as said below
- conv_in: float32 [3, 16, 4], replicated, may hold values from -1.75 to 1.75
- bias_in: float32 [16], replicated, may hold values from -3 to 3
- conv_out: float32 [3, 2, 16], replicated, may hold values from -0.875 to 0.875
- bias_out: float32 [2], replicated, may hold values from -3 to 3
Outputs:
- tracer_next: float32 [2, 48, 16, 4096], P(None, 'lev', None, ('grp', 'elem')), parts along dimension 3
- subgrid: float32 [2, 48, 4, 4096], P(None, 'lev', None, ('grp', 'elem')), parts along dimension 3
The draws below stay inside these ranges and needn't reach their ends.
There are 2 independent parts, one for each index of `grp`. The reference program is written for one: setup_inputs(seed, part) draws one part's arguments, and reference() takes and returns one part's arrays. A program takes and returns all parts, laid end to end along the dimension named above; an argument that names none is the same for every part. Nothing has to cross between parts.
Inputs may be any that keep to these rules, and one draw needn't show every extreme that they name: Across edge k, element e touches edge (k + 2) mod 4 of element neighbours[k, e], and neighbours[(k + 2) mod 4, neighbours[k, e]] is e. Elements are numbered so that index j of elem owns elements j * 256 to (j + 1) * 256 - 1; the neighbours across edges 1 and 3 are owned by the same index of elem, those across edges 0 and 2 by the same index or the next or previous one, cyclically; across edge 0 never the next one and across edge 2 never the previous one. seam_flips[k, e] equals seam_flips[(k + 2) mod 4, neighbours[k, e]].
All inputs are finite; a program needn't handle non-finite values.
Results may differ from the reference program's by a relative error of at most 0.0001.
Values sent between devices are 32-bit elements; how exact they have to be, the bound alone decides.
A program may use at most 64 MiB of HBM per device.

```python
import math
import jax
import jax.numpy as jnp
import numpy as np
from jax import lax

TRACERS = 2
NODES = 16
LEVELS = 48
FEATURES = 4
CHANNELS = 16
ROW_ELEMS = 256
ELEM_DEV = 256
ELEMS = 2048


def grid_tables(key):
    rows_total = ELEMS // ROW_ELEMS
    blocks = ELEMS // ELEM_DEV
    keys = jax.random.split(jax.random.fold_in(key, 11), blocks)

    def block_order(block_key):
        return jax.random.permutation(block_key, ELEM_DEV).astype(jnp.int32)
    orders = jax.vmap(block_order)(keys)
    labels = (jnp.arange(blocks, dtype=jnp.int32)[:, None] * ELEM_DEV + orders).reshape(-1)
    cell_of = jnp.zeros((ELEMS,), jnp.int32).at[labels].set(jnp.arange(ELEMS, dtype=jnp.int32))
    row_of = cell_of // ROW_ELEMS
    col_of = cell_of % ROW_ELEMS

    def at_cell(row_value, col_value):
        return labels[row_value % rows_total * ROW_ELEMS + col_value % ROW_ELEMS]
    to_south = at_cell(row_of - 1, col_of)
    to_east = at_cell(row_of, col_of + 1)
    to_north = at_cell(row_of + 1, col_of)
    to_west = at_cell(row_of, col_of - 1)
    across = jax.random.randint(jax.random.fold_in(key, 12), (rows_total, ROW_ELEMS), 0, 2).astype(jnp.int32)
    upward = jax.random.randint(jax.random.fold_in(key, 13), (rows_total, ROW_ELEMS), 0, 2).astype(jnp.int32)
    flip_south = upward[(row_of - 1) % rows_total, col_of]
    flip_east = across[row_of, col_of]
    flip_north = upward[row_of, col_of]
    flip_west = across[row_of, (col_of - 1) % ROW_ELEMS]
    neighbour_table = jnp.stack([to_south, to_east, to_north, to_west]).astype(jnp.int32)
    flip_table = jnp.stack([flip_south, flip_east, flip_north, flip_west]).astype(jnp.int32)
    return (neighbour_table, flip_table)


def draw_neighbours(key, part):
    return grid_tables(key)[0]


def draw_seam_flips(key, part):
    return grid_tables(key)[1]


def steps_of(rng, extent, shards, least, largest):
    def one(dim, shards_of):
        draws = jax.random.uniform(jax.random.fold_in(jax.random.fold_in(rng, 6), dim), (shards_of,), jnp.float32, least / len(shards), largest / len(shards))
        return jnp.repeat(jnp.exp(draws), extent[dim] // shards_of).reshape((-1,) + (1,) * (len(extent) - dim - 1))

    loudness = one(*shards[0])
    for cut in shards[1:]:
        loudness = loudness * one(*cut)
    return loudness


def noise(key, extent, spread, reach, cuts=(), kind=jnp.bfloat16):
    entries = jax.random.normal(key, extent, jnp.float32) * spread
    if len(cuts) > 0:
        entries = steps_of(key, extent, cuts, -0.22, 0.18) * entries
    return jnp.clip(entries, min=-reach, max=reach).astype(kind)


def setup_inputs(seed: int = 0, part: int = 0) -> dict:
    streams_of = jax.random.split(jax.random.key(seed), 10)
    own_keys = jax.random.split(jax.random.fold_in(streams_of[9], part), 10)
    return {
        "tracer_field": noise(own_keys[0], (TRACERS, LEVELS, NODES, ELEMS), 1.0, 6.0, ((1, 2), (3, 8)), jnp.float32),
        "velocity": noise(own_keys[1], (2, LEVELS, NODES, ELEMS), 0.7, 3.0, ((1, 2), (3, 8)), jnp.float32),
        "node_mass": jnp.clip(jnp.exp(math.log(2.0) - 1.3862944 * jax.random.uniform(own_keys[2], (NODES, ELEMS), jnp.float32) ** steps_of(own_keys[2], (NODES, ELEMS), ((1, 8),), -0.2, 0.2)), 0.5, 2.0),
        "neighbours": draw_neighbours(jax.random.fold_in(jax.random.fold_in(streams_of[9], part), 71), part),
        "seam_flips": draw_seam_flips(jax.random.fold_in(jax.random.fold_in(streams_of[9], part), 71), part),
        "conv_in": noise(streams_of[5], (3, CHANNELS, FEATURES), (3 * FEATURES) ** -0.5, 1.75, (), jnp.float32),
        "bias_in": noise(streams_of[6], (CHANNELS,), 0.5, 3.0, (), jnp.float32),
        "conv_out": noise(streams_of[7], (3, TRACERS, CHANNELS), (3 * CHANNELS) ** -0.5, 0.875, (), jnp.float32),
        "bias_out": noise(streams_of[8], (TRACERS,), 0.5, 3.0, (), jnp.float32),
    }


TIME_STEP = 0.1
EDGE_NODES = ((0, 1, 2, 3), (3, 7, 11, 15), (12, 13, 14, 15), (0, 4, 8, 12))

def derivative_tables():
    gll_points = np.array([-1.0, -1.0 / np.sqrt(5.0), 1.0 / np.sqrt(5.0), 1.0])
    barycentric = np.array([1.0 / np.prod([gll_points[row_index] - gll_points[other_index] for other_index in range(4) if other_index != row_index]) for row_index in range(4)])
    matrix = np.zeros((4, 4))
    for row_index in range(4):
        for col_index in range(4):
            if row_index != col_index:
                matrix[row_index, col_index] = barycentric[col_index] / barycentric[row_index] / (gll_points[row_index] - gll_points[col_index])
        matrix[row_index, row_index] = -np.sum(matrix[row_index])
    identity = np.eye(4)
    return (jnp.asarray(np.kron(identity, matrix), dtype=jnp.float32), jnp.asarray(np.kron(matrix, identity), dtype=jnp.float32))

def cell_table():
    table = np.zeros((4, 16))
    for node_index in range(16):
        table[2 * (node_index // 4 // 2) + node_index % 4 // 2, node_index] = 1.0
    return jnp.asarray(table, dtype=jnp.float32)

def edge_average(values, node_mass, neighbours, seam_flips):
    weighted = values * node_mass
    summed = weighted
    total_mass = node_mass
    for side_index in range(4):
        own_nodes = np.array(EDGE_NODES[side_index])
        their_nodes = np.array(EDGE_NODES[(side_index + 2) % 4])
        flipped = seam_flips[side_index] == 1
        arrived = jnp.take(weighted[:, :, their_nodes, :], neighbours[side_index], axis=3)
        arrived = jnp.where(flipped[None, None, None, :], arrived[:, :, ::-1, :], arrived)
        arrived_mass = jnp.take(node_mass[their_nodes], neighbours[side_index], axis=1)
        arrived_mass = jnp.where(flipped[None, :], arrived_mass[::-1], arrived_mass)
        summed = summed.at[:, :, own_nodes, :].add(arrived)
        total_mass = total_mass.at[own_nodes].add(arrived_mass)
    return summed / total_mass

def tendency(values, velocity, node_mass, neighbours, seam_flips):
    deriv_x, deriv_y = derivative_tables()
    slope_x = jnp.einsum('mn,tlne->tlme', deriv_x, values, precision=lax.Precision.HIGHEST)
    slope_y = jnp.einsum('mn,tlne->tlme', deriv_y, values, precision=lax.Precision.HIGHEST)
    return edge_average(-(velocity[0] * slope_x + velocity[1] * slope_y), node_mass, neighbours, seam_flips)

def to_cells(values, node_mass):
    table = cell_table()
    summed = jnp.einsum('cn,tlne->tlce', table, values * node_mass, precision=lax.Precision.HIGHEST)
    weight = jnp.dot(table, node_mass, precision=lax.Precision.HIGHEST)
    return summed / weight

def valid_conv(padded, kernel, bias):
    count = padded.shape[1] - 2
    result = jnp.zeros((kernel.shape[1], count, padded.shape[2], padded.shape[3]), jnp.float32) + bias[:, None, None, None]
    for offset in range(3):
        result = result + jnp.einsum('oi,ilce->olce', kernel[offset], lax.slice_in_dim(padded, offset, offset + count, axis=1), precision=lax.Precision.HIGHEST)
    return result

def convolve(signal, kernel, bias):
    return valid_conv(jnp.pad(signal, ((0, 0), (1, 1), (0, 0), (0, 0))), kernel, bias)

def reference(tracer_field, velocity, node_mass, neighbours, seam_flips, conv_in, bias_in, conv_out, bias_out):
    section = tracer_field + TIME_STEP * tendency(tracer_field, velocity, node_mass, neighbours, seam_flips)
    section = 0.75 * tracer_field + 0.25 * (section + TIME_STEP * tendency(section, velocity, node_mass, neighbours, seam_flips))
    tracer_next = tracer_field / 3.0 + 2.0 / 3.0 * (section + TIME_STEP * tendency(section, velocity, node_mass, neighbours, seam_flips))
    features = jnp.concatenate([to_cells(tracer_next, node_mass), to_cells(velocity, node_mass)], axis=0)
    hidden = jax.nn.silu(convolve(features, conv_in, bias_in))
    subgrid = convolve(hidden, conv_out, bias_out)
    return (tracer_next, subgrid)
```

```python
import functools

import jax
import jax.numpy as jnp
import numpy as np
from jax import lax
from jax.experimental import pallas as pl
from jax.experimental.pallas import tpu as pltpu
from jax.sharding import PartitionSpec as P

TIME_STEP = 0.1
EDGE_NODES = ((0, 1, 2, 3), (3, 7, 11, 15), (12, 13, 14, 15), (0, 4, 8, 12))
MESH = pl.DeviceIdType.MESH
SUB = 8
GUARD = 16


def derivative_matrix():
    points = np.array([-1.0, -1.0 / np.sqrt(5.0), 1.0 / np.sqrt(5.0), 1.0])
    bary = [
        1.0 / np.prod([points[i] - points[k] for k in range(4) if k != i]) for i in range(4)
    ]
    matrix = np.zeros((4, 4))
    for i in range(4):
        for j in range(4):
            if i != j:
                matrix[i, j] = bary[j] / bary[i] / (points[i] - points[j])
        matrix[i, i] = -np.sum(matrix[i])
    matrix[np.abs(matrix) < 1e-12] = 0.0
    return matrix


def gathered(values, table, parts):
    rows = values.shape[0]
    pieces, rest = [], values
    for _ in range(parts):
        piece = rest.astype(jnp.bfloat16)
        pieces.append(piece)
        rest = rest - piece.astype(jnp.float32)
    out = jnp.dot(jnp.concatenate(pieces, axis=0), table, preferred_element_type=jnp.float32)
    total = out[:rows]
    for part in range(1, parts):
        total = total + out[part * rows : (part + 1) * rows]
    return total


def kernel(
    devices, tracer_in, velocity_in, mass, nbr, flips, conv_in, bias_in, conv_out, bias_out,
    next_out, sub_out,
    start, now, wind, weighted, base, landed, inv, cell_inv, tables, mass_land, features, partial,
    in_sem, send_sem, recv_sem, mass_send_sem, mass_recv_sem, col_send_sem, col_recv_sem,
):
    local = mass.shape[1]
    levels = start.shape[2]
    chunks = levels // SUB
    matrix = derivative_matrix()
    me, lev = lax.axis_index("elem"), lax.axis_index("lev")
    after, before = lax.rem(me + 1, devices), lax.rem(me + devices - 1, devices)

    loads = []
    for node in range(16):
        loads.append(
            pltpu.make_async_copy(tracer_in.at[:, :, node, :], start.at[node], in_sem.at[0, node])
        )
        loads.append(
            pltpu.make_async_copy(velocity_in.at[:, :, node, :], wind.at[node], in_sem.at[1, node])
        )
    for load in loads:
        load.start()

    barrier = pltpu.get_barrier_semaphore()
    for device in ({"elem": before}, {"elem": after}, {"lev": 1 - lev}):
        pl.semaphore_signal(barrier, inc=1, device_id=device, device_id_type=MESH)

    rows = lax.broadcasted_iota(jnp.int32, (local, local), 0)
    for slot, (edge, owner) in enumerate(
        ((0, me), (1, me), (2, me), (3, me), (0, before), (2, after))
    ):
        wanted = nbr[pl.ds(edge, 1), :] - owner * local
        tables[slot] = jnp.where(rows == wanted, 1.0, 0.0).astype(jnp.bfloat16)
    pl.semaphore_wait(barrier, 3)

    mass_copies = []
    for side, device in ((0, after), (1, before)):
        mass_copies.append(
            pltpu.make_async_remote_copy(
                src_ref=mass.at[pl.ds(8 * (1 - side), 8), :],
                dst_ref=mass_land.at[side],
                send_sem=mass_send_sem.at[side],
                recv_sem=mass_recv_sem.at[side],
                device_id={"elem": device},
                device_id_type=MESH,
            )
        )
        mass_copies[-1].start()

    def edge_copy(side, step):
        return pltpu.make_async_remote_copy(
            src_ref=weighted.at[step, pl.ds(12 if side == 0 else 0, 4)],
            dst_ref=landed.at[side, step],
            send_sem=send_sem.at[side, step],
            recv_sem=recv_sem.at[side, step],
            device_id={"elem": after if side == 0 else before},
            device_id_type=MESH,
        )

    def place(chunk):
        return pl.multiple_of(jnp.where(lev == 0, chunks - 1 - chunk, chunk) * SUB, SUB)

    def is_flipped(edge):
        return flips[pl.ds(edge, 1), :] == 1

    def slopes(field, chunk, step):
        at = pl.ds(place(chunk), SUB)
        for tracer in range(2):
            q = [field[node, tracer, at, :] for node in range(16)]
            for node in (12, 13, 14, 15, 0, 1, 2, 3, 4, 5, 6, 7, 8, 9, 10, 11):
                iy, ix = divmod(node, 4)
                along_x = sum(float(matrix[ix, j]) * q[4 * iy + j] for j in range(4) if matrix[ix, j])
                along_y = sum(float(matrix[iy, j]) * q[4 * j + ix] for j in range(4) if matrix[iy, j])
                weighted[step, node, tracer] = (
                    wind[node, 0, at, :] * along_x + wind[node, 1, at, :] * along_y
                )
        edge_copy(0, step).start()
        edge_copy(1, step).start()
        arrivals = [[] for _ in range(16)]
        for edge in range(4):
            theirs = EDGE_NODES[(edge + 2) % 4]
            source = jnp.concatenate(
                [weighted[step, node].reshape(2 * SUB, local) for node in theirs], axis=0
            )
            settle(arrivals, edge, gathered(source, tables[edge], 2))
        for node in range(16):
            total = weighted[step, node].reshape(2 * SUB, local)
            for arrived in arrivals[node]:
                total = total + arrived
            base[chunk, node] = total.reshape(2, SUB, local)

    def settle(arrivals, edge, arrived):
        count = arrived.shape[0] // 4
        flip = is_flipped(edge)
        for slot, node in enumerate(EDGE_NODES[edge]):
            arrivals[node].append(
                jnp.where(
                    flip,
                    arrived[(3 - slot) * count : (4 - slot) * count],
                    arrived[slot * count : (slot + 1) * count],
                )
            )

    def finish(chunk, step, keep, blend):
        at = pl.ds(place(chunk), SUB)
        edge_copy(0, step).wait_recv()
        edge_copy(1, step).wait_recv()
        arrivals = [[] for _ in range(16)]
        for side, edge in ((0, 0), (1, 2)):
            source = landed[side, step].reshape(8 * SUB, local)
            settle(arrivals, edge, gathered(source, tables[4 + side], 2))
        for node in range(16):
            total = base[chunk, node].reshape(2 * SUB, local)
            for arrived in arrivals[node]:
                total = total + arrived
            total = total.reshape(2, SUB, local)
            for tracer in range(2):
                section = now[node, tracer, at, :] + TIME_STEP * inv[node] * total[tracer]
                now[node, tracer, at, :] = keep * start[node, tracer, at, :] + blend * section

    for load in loads:
        load.wait()

    def prepare(chunk, carry):
        at = pl.ds(place(chunk), SUB)
        for node in range(16):
            node_mass = mass[pl.ds(node, 1), :]
            for way in range(2):
                wind[node, way, at, :] = -(wind[node, way, at, :] * node_mass)
            for tracer in range(2):
                now[node, tracer, at, :] = start[node, tracer, at, :]
        slopes(start, chunk, chunk)
        return carry

    lax.fori_loop(0, chunks, prepare, 0)

    own_mass = mass[...]
    sums = [own_mass[node : node + 1] for node in range(16)]
    own = [
        gathered(own_mass[8:16], tables[0], 3),
        gathered(own_mass, tables[1], 3),
        gathered(own_mass[0:8], tables[2], 3),
        gathered(own_mass, tables[3], 3),
    ]
    for side in range(2):
        mass_copies[side].wait_recv()
    far = [gathered(mass_land[side], tables[4 + side], 3) for side in range(2)]
    own[0] = own[0] + far[0]
    own[2] = own[2] + far[1]
    for edge in range(4):
        theirs = EDGE_NODES[(edge + 2) % 4]
        shift = 8 if edge == 0 else 0
        flip = is_flipped(edge)
        for slot, node in enumerate(EDGE_NODES[edge]):
            straight, turned = theirs[slot] - shift, theirs[3 - slot] - shift
            sums[node] = sums[node] + jnp.where(
                flip, own[edge][turned : turned + 1], own[edge][straight : straight + 1]
            )
    for node in range(16):
        inv[node] = jnp.broadcast_to(1.0 / sums[node], (SUB, local))
    cells = [
        [4 * (2 * (cell // 2) + dy) + 2 * (cell % 2) + dx for dy in range(2) for dx in range(2)]
        for cell in range(4)
    ]
    for cell in range(4):
        cell_mass = sum(own_mass[node : node + 1] for node in cells[cell])
        cell_inv[cell] = jnp.broadcast_to(1.0 / cell_mass, (SUB, local))

    nothing = jnp.zeros((SUB, local), jnp.float32)
    open_side = pl.multiple_of(jnp.where(lev == 0, GUARD - SUB, GUARD + levels), SUB)
    for cell in range(4):
        for channel in range(4):
            features[channel, cell, pl.ds(0, SUB), :] = nothing
            features[channel, cell, pl.ds(GUARD + levels + SUB, SUB), :] = nothing
            features[channel, cell, pl.ds(open_side, SUB), :] = nothing
        for kind in range(6):
            partial[kind, cell, pl.ds(open_side, SUB), :] = nothing

    def section_step(index, carry):
        chunk = lax.rem(index, chunks)
        first, second = index < chunks, index < 2 * chunks
        keep = jnp.where(first, 0.0, jnp.where(second, 0.75, 1.0 / 3.0)).astype(jnp.float32)
        blend = jnp.where(first, 1.0, jnp.where(second, 0.25, 2.0 / 3.0)).astype(jnp.float32)
        finish(chunk, index, keep, blend)

        @pl.when(second)
        def _():
            slopes(now, chunk, index + chunks)

        return carry

    lax.fori_loop(0, 2 * chunks, section_step, 0)

    column_copy = pltpu.make_async_remote_copy(
        src_ref=features.at[:, :, pl.ds(pl.multiple_of(GUARD + place(0), SUB), SUB), :],
        dst_ref=features.at[
            :, :, pl.ds(pl.multiple_of(jnp.where(lev == 0, GUARD - SUB, GUARD + levels), SUB), SUB), :
        ],
        send_sem=col_send_sem,
        recv_sem=col_recv_sem,
        device_id={"lev": 1 - lev},
        device_id_type=MESH,
    )

    def last_step(index, carry):
        chunk = index - 2 * chunks
        finish(chunk, index, jnp.float32(1.0 / 3.0), jnp.float32(2.0 / 3.0))
        at = pl.ds(place(chunk), SUB)
        column = pl.ds(pl.multiple_of(GUARD + place(chunk), SUB), SUB)
        for cell in range(4):
            for tracer in range(2):
                features[tracer, cell, column, :] = cell_inv[cell] * sum(
                    mass[pl.ds(node, 1), :] * now[node, tracer, at, :] for node in cells[cell]
                )
                features[2 + tracer, cell, column, :] = -cell_inv[cell] * sum(
                    wind[node, tracer, at, :] for node in cells[cell]
                )
        for node in range(16):
            for tracer in range(2):
                next_out[node, tracer, at, :] = now[node, tracer, at, :]

        @pl.when(chunk == 0)
        def _():
            column_copy.start()

        return carry

    lax.fori_loop(2 * chunks, 3 * chunks, last_step, 0)
    column_copy.wait()

    def column_net(index, carry):
        chunk, cell = index // 4, lax.rem(index, 4)
        inner = GUARD + chunk * SUB
        border = jnp.where(lev == 0, GUARD + levels, GUARD - SUB)
        at = pl.multiple_of(jnp.where(chunk < chunks, inner, border), SUB)
        inputs = []
        for channel in range(4):
            whole = features[channel, cell, pl.ds(pl.multiple_of(at - SUB, SUB), 3 * SUB), :]
            inputs.append([whole[SUB - 1 + j : 2 * SUB - 1 + j] for j in range(3)])
        totals = [None] * 6
        for out in range(16):
            value = bias_in[out]
            for j in range(3):
                for channel in range(4):
                    value = value + conv_in[j, out, channel] * inputs[channel][j]
            value = value / (1.0 + jnp.exp(-value))
            for j in range(3):
                for tracer in range(2):
                    term = conv_out[j, tracer, out] * value
                    kind = 2 * j + tracer
                    totals[kind] = term if totals[kind] is None else totals[kind] + term
        for kind in range(6):
            partial[kind, cell, pl.ds(at, SUB), :] = totals[kind]
        return carry

    lax.fori_loop(0, 4 * (chunks + 1), column_net, 0)

    for cell in range(4):
        for tracer in range(2):
            sub_out[tracer, cell] = (
                bias_out[tracer]
                + partial[tracer, cell, pl.ds(GUARD - 1, levels), :]
                + partial[2 + tracer, cell, pl.ds(GUARD, levels), :]
                + partial[4 + tracer, cell, pl.ds(GUARD + 1, levels), :]
            )

    def drain(index, carry):
        edge_copy(0, index).wait_send()
        edge_copy(1, index).wait_send()
        return carry

    lax.fori_loop(0, 3 * chunks, drain, 0)
    for side in range(2):
        mass_copies[side].wait_send()


def per_device(
    tracer_field, velocity, node_mass, neighbours, seam_flips, conv_in, bias_in, conv_out, bias_out
):
    devices = lax.axis_size("elem")
    tracers, levels, nodes, local = tracer_field.shape
    steps = 3 * (levels // SUB)
    f32 = jnp.float32
    vmem = pl.BlockSpec(memory_space=pltpu.VMEM)
    smem = pl.BlockSpec(memory_space=pltpu.SMEM)
    hbm = pl.BlockSpec(memory_space=pl.ANY)
    tall = levels + 2 * GUARD
    by_node, by_cell = pl.pallas_call(
        functools.partial(kernel, devices),
        out_shape=(
            jax.ShapeDtypeStruct((nodes, tracers, levels, local), f32),
            jax.ShapeDtypeStruct((tracers, 4, levels, local), f32),
        ),
        in_specs=[hbm, hbm, vmem, vmem, vmem, smem, smem, smem, smem],
        out_specs=(vmem, vmem),
        scratch_shapes=[
            pltpu.VMEM((nodes, tracers, levels, local), f32),
            pltpu.VMEM((nodes, tracers, levels, local), f32),
            pltpu.VMEM((nodes, 2, levels, local), f32),
            pltpu.VMEM((steps, nodes, tracers, SUB, local), f32),
            pltpu.VMEM((steps // 3, nodes, tracers, SUB, local), f32),
            pltpu.VMEM((2, steps, 4, tracers, SUB, local), f32),
            pltpu.VMEM((nodes, SUB, local), f32),
            pltpu.VMEM((4, SUB, local), f32),
            pltpu.VMEM((6, local, local), jnp.bfloat16),
            pltpu.VMEM((2, 8, local), f32),
            pltpu.VMEM((4, 4, tall, local), f32),
            pltpu.VMEM((6, 4, tall, local), f32),
            pltpu.SemaphoreType.DMA((2, nodes)),
            pltpu.SemaphoreType.DMA((2, steps)),
            pltpu.SemaphoreType.DMA((2, steps)),
            pltpu.SemaphoreType.DMA((2,)),
            pltpu.SemaphoreType.DMA((2,)),
            pltpu.SemaphoreType.DMA,
            pltpu.SemaphoreType.DMA,
        ],
        compiler_params=pltpu.CompilerParams(
            collective_id=0, has_side_effects=True, vmem_limit_bytes=40 * 2**20
        ),
    )(
        tracer_field, velocity, node_mass, neighbours, seam_flips,
        conv_in, bias_in, conv_out, bias_out,
    )
    return jnp.transpose(by_node, (1, 2, 0, 3)), jnp.transpose(by_cell, (0, 2, 1, 3))


def solution(mesh):
    return jax.shard_map(
        per_device,
        mesh=mesh,
        in_specs=(
            P(None, "lev", None, ("grp", "elem")),
            P(None, "lev", None, ("grp", "elem")),
            P(None, ("grp", "elem")),
            P(None, ("grp", "elem")),
            P(None, ("grp", "elem")),
            P(),
            P(),
            P(),
            P(),
        ),
        out_specs=(P(None, "lev", None, ("grp", "elem")), P(None, "lev", None, ("grp", "elem"))),
        check_vma=False,
    )
```

```python
import functools

import jax
import jax.numpy as jnp
import numpy as np
from jax import lax
from jax.experimental import pallas as pl
from jax.experimental.pallas import tpu as pltpu
from jax.sharding import PartitionSpec as P

TIME_STEP = 0.1
EDGE_NODES = ((0, 1, 2, 3), (3, 7, 11, 15), (12, 13, 14, 15), (0, 4, 8, 12))
MESH = pl.DeviceIdType.MESH
SUB = 8
GUARD = 16


def derivative_matrix():
    points = np.array([-1.0, -1.0 / np.sqrt(5.0), 1.0 / np.sqrt(5.0), 1.0])
    bary = [
        1.0 / np.prod([points[i] - points[k] for k in range(4) if k != i]) for i in range(4)
    ]
    matrix = np.zeros((4, 4))
    for i in range(4):
        for j in range(4):
            if i != j:
                matrix[i, j] = bary[j] / bary[i] / (points[i] - points[j])
        matrix[i, i] = -np.sum(matrix[i])
    matrix[np.abs(matrix) < 1e-12] = 0.0
    return matrix


def gathered(values, table, parts):
    rows = values.shape[0]
    pieces, rest = [], values
    for _ in range(parts):
        piece = rest.astype(jnp.bfloat16)
        pieces.append(piece)
        rest = rest - piece.astype(jnp.float32)
    out = jnp.dot(jnp.concatenate(pieces, axis=0), table, preferred_element_type=jnp.float32)
    total = out[:rows]
    for part in range(1, parts):
        total = total + out[part * rows : (part + 1) * rows]
    return total


def kernel(
    devices, tracer_in, velocity_in, mass, nbr, flips, conv_in, bias_in, conv_out, bias_out,
    next_out, sub_out,
    start, now, wind, weighted, base, landed, inv, cell_inv, tables, mass_land, features, totals,
    first_net, second_net, in_sem, send_sem, recv_sem, mass_send_sem, mass_recv_sem, col_send_sem, col_recv_sem,
):
    local = mass.shape[1]
    levels = start.shape[2]
    chunks = levels // SUB
    matrix = derivative_matrix()
    me, lev = lax.axis_index("elem"), lax.axis_index("lev")
    after, before = lax.rem(me + 1, devices), lax.rem(me + devices - 1, devices)

    def place(chunk):
        return pl.multiple_of(jnp.where(lev == 0, chunks - 1 - chunk, chunk) * SUB, SUB)

    def load_copies(chunk):
        at = pl.ds(place(chunk), SUB)
        return [
            pltpu.make_async_copy(
                source.at[:, at, node, :], target.at[node, :, at, :], in_sem.at[chunk, kind, node]
            )
            for kind, (source, target) in enumerate(((tracer_in, start), (velocity_in, wind)))
            for node in range(16)
        ]

    def load(chunk, carry):
        for copy in load_copies(chunk):
            copy.start()
        return carry

    barrier = pltpu.get_barrier_semaphore()
    for device in ({"elem": before}, {"elem": after}, {"lev": 1 - lev}):
        pl.semaphore_signal(barrier, inc=1, device_id=device, device_id_type=MESH)
    lax.fori_loop(0, chunks, load, 0)

    mass_copies = []
    for side, device in ((0, after), (1, before)):
        mass_copies.append(
            pltpu.make_async_remote_copy(
                src_ref=mass.at[pl.ds(8 * (1 - side), 8), :],
                dst_ref=mass_land.at[side],
                send_sem=mass_send_sem.at[side],
                recv_sem=mass_recv_sem.at[side],
                device_id={"elem": device},
                device_id_type=MESH,
            )
        )

    def edge_copy(side, step):
        return pltpu.make_async_remote_copy(
            src_ref=weighted.at[step, pl.ds(12 if side == 0 else 0, 4)],
            dst_ref=landed.at[side, step],
            send_sem=send_sem.at[side, step],
            recv_sem=recv_sem.at[side, step],
            device_id={"elem": after if side == 0 else before},
            device_id_type=MESH,
        )

    def is_flipped(edge):
        return flips[pl.ds(edge, 1), :] == 1

    def slopes(field, chunk, step):
        at = pl.ds(place(chunk), SUB)
        for tracer in range(2):
            q = [field[node, tracer, at, :] for node in range(16)]
            for node in (12, 13, 14, 15, 0, 1, 2, 3, 4, 5, 6, 7, 8, 9, 10, 11):
                iy, ix = divmod(node, 4)
                along_x = sum(float(matrix[ix, j]) * q[4 * iy + j] for j in range(4) if matrix[ix, j])
                along_y = sum(float(matrix[iy, j]) * q[4 * j + ix] for j in range(4) if matrix[iy, j])
                weighted[step, node, tracer] = (
                    wind[node, 0, at, :] * along_x + wind[node, 1, at, :] * along_y
                )

    def send(step):
        edge_copy(0, step).start()
        edge_copy(1, step).start()

    def gather_local(chunk, step):
        arrivals = [[] for _ in range(16)]
        for edge in range(4):
            theirs = EDGE_NODES[(edge + 2) % 4]
            source = jnp.concatenate(
                [weighted[step, node].reshape(2 * SUB, local) for node in theirs], axis=0
            )
            settle(arrivals, edge, gathered(source, tables[edge], 2))
        for node in range(16):
            total = weighted[step, node].reshape(2 * SUB, local)
            for arrived in arrivals[node]:
                total = total + arrived
            base[chunk, node] = total.reshape(2, SUB, local)

    def settle(arrivals, edge, arrived):
        count = arrived.shape[0] // 4
        flip = is_flipped(edge)
        for slot, node in enumerate(EDGE_NODES[edge]):
            arrivals[node].append(
                jnp.where(
                    flip,
                    arrived[(3 - slot) * count : (4 - slot) * count],
                    arrived[slot * count : (slot + 1) * count],
                )
            )

    def finish(chunk, step, keep, blend):
        at = pl.ds(place(chunk), SUB)
        edge_copy(0, step).wait_recv()
        edge_copy(1, step).wait_recv()
        arrivals = [[] for _ in range(16)]
        for side, edge in ((0, 0), (1, 2)):
            source = landed[side, step].reshape(8 * SUB, local)
            settle(arrivals, edge, gathered(source, tables[4 + side], 2))
        for node in range(16):
            total = base[chunk, node].reshape(2 * SUB, local)
            for arrived in arrivals[node]:
                total = total + arrived
            total = total.reshape(2, SUB, local)
            for tracer in range(2):
                section = now[node, tracer, at, :] + TIME_STEP * inv[node] * total[tracer]
                now[node, tracer, at, :] = keep * start[node, tracer, at, :] + blend * section

    def prepare(chunk):
        for copy in load_copies(chunk):
            copy.wait()
        at = pl.ds(place(chunk), SUB)
        for node in range(16):
            node_mass = mass[pl.ds(node, 1), :]
            for way in range(2):
                wind[node, way, at, :] = -(wind[node, way, at, :] * node_mass)
            for tracer in range(2):
                now[node, tracer, at, :] = start[node, tracer, at, :]
        slopes(start, chunk, chunk)

    prepare(0)
    pl.semaphore_wait(barrier, 3)
    for copy in mass_copies:
        copy.start()
    send(0)

    def prepare_next(chunk, carry):
        prepare(chunk)
        send(chunk)
        return carry

    lax.fori_loop(1, chunks, prepare_next, 0)

    rows = lax.broadcasted_iota(jnp.int32, (local, local), 0)
    for slot, (edge, owner) in enumerate(
        ((0, me), (1, me), (2, me), (3, me), (0, before), (2, after))
    ):
        wanted = nbr[pl.ds(edge, 1), :] - owner * local
        tables[slot] = jnp.where(rows == wanted, 1.0, 0.0).astype(jnp.bfloat16)

    def gather_first(chunk, carry):
        gather_local(chunk, chunk)
        return carry

    lax.fori_loop(0, chunks, gather_first, 0)

    own_mass = mass[...]
    sums = [own_mass[node : node + 1] for node in range(16)]
    own = [
        gathered(own_mass[8:16], tables[0], 3),
        gathered(own_mass, tables[1], 3),
        gathered(own_mass[0:8], tables[2], 3),
        gathered(own_mass, tables[3], 3),
    ]
    for side in range(2):
        mass_copies[side].wait_recv()
    far = [gathered(mass_land[side], tables[4 + side], 3) for side in range(2)]
    own[0] = own[0] + far[0]
    own[2] = own[2] + far[1]
    for edge in range(4):
        theirs = EDGE_NODES[(edge + 2) % 4]
        shift = 8 if edge == 0 else 0
        flip = is_flipped(edge)
        for slot, node in enumerate(EDGE_NODES[edge]):
            straight, turned = theirs[slot] - shift, theirs[3 - slot] - shift
            sums[node] = sums[node] + jnp.where(
                flip, own[edge][turned : turned + 1], own[edge][straight : straight + 1]
            )
    for node in range(16):
        inv[node] = jnp.broadcast_to(1.0 / sums[node], (SUB, local))
    cells = [
        [4 * (2 * (cell // 2) + dy) + 2 * (cell % 2) + dx for dy in range(2) for dx in range(2)]
        for cell in range(4)
    ]
    for cell in range(4):
        cell_mass = sum(own_mass[node : node + 1] for node in cells[cell])
        cell_inv[cell] = jnp.broadcast_to(1.0 / cell_mass, (SUB, local))

    def clear_columns():
        nothing = jnp.zeros((SUB, local), jnp.float32)
        open_side = pl.multiple_of(jnp.where(lev == 0, GUARD - SUB, GUARD + levels), SUB)
        for cell in range(4):
            for channel in range(4):
                features[channel, cell, pl.ds(0, SUB), :] = nothing
                features[channel, cell, pl.ds(GUARD + levels + SUB, SUB), :] = nothing
                features[channel, cell, pl.ds(open_side, SUB), :] = nothing
            for tracer in range(2):
                totals[tracer, cell] = jnp.full(totals.shape[2:], bias_out[tracer], jnp.float32)

    wide, deep = 4 * 3 * SUB, 16 * SUB

    def split(table, columns):
        second = lax.broadcasted_iota(jnp.int32, table.shape, 1) >= columns
        high = table.astype(jnp.bfloat16)
        low = jnp.where(second, 0.0, table - high.astype(jnp.float32)).astype(jnp.bfloat16)
        return high, low

    def build_nets():
        col = lax.rem(lax.broadcasted_iota(jnp.int32, (SUB, 2 * wide), 1), wide)
        row = lax.broadcasted_iota(jnp.int32, (SUB, 2 * wide), 0)
        reach = lax.rem(col, 3 * SUB) - row - (SUB - 1)
        masks = [
            [jnp.where((reach == j) & (col // (3 * SUB) == i), 1.0, 0.0) for i in range(4)]
            for j in range(3)
        ]
        for out in range(0, 16, 2):
            pair = [
                sum(conv_in[j, i, o] * masks[j][i] for j in range(3) for i in range(4))
                for o in (out, out + 1)
            ]
            high, low = split(jnp.concatenate(pair, axis=0), wide)
            first_net[pl.ds(SUB * out, 2 * SUB), :] = high
            first_net[pl.ds(deep + SUB * out, 2 * SUB), :] = low
        col = lax.rem(lax.broadcasted_iota(jnp.int32, (3 * SUB, 2 * deep), 1), deep)
        row = lax.broadcasted_iota(jnp.int32, (3 * SUB, 2 * deep), 0)
        reach = SUB + 1 + lax.rem(col, SUB) - row
        bands = []
        for tracer in range(2):
            band = jnp.zeros((3 * SUB, 2 * deep), jnp.float32)
            for o in range(16):
                weight = jnp.zeros((3 * SUB, 2 * deep), jnp.float32)
                for j in range(3):
                    weight = jnp.where(reach == j, conv_out[j, tracer, o], weight)
                band = jnp.where(col // SUB == o, weight, band)
            bands.append(band)
        high, low = split(jnp.concatenate(bands, axis=0), deep)
        second_net[pl.ds(0, 6 * SUB), :] = high
        second_net[pl.ds(6 * SUB, 6 * SUB), :] = low

    def applied(net, values):
        high = values.astype(jnp.bfloat16)
        low = (values - high.astype(jnp.float32)).astype(jnp.bfloat16)
        both = jnp.dot(
            net[...], jnp.concatenate([high, low], axis=0), preferred_element_type=jnp.float32
        )
        half = both.shape[0] // 2
        return both[:half] + both[half:]

    def column_net(at):
        window = pl.ds(pl.multiple_of(at - SUB, SUB), 3 * SUB)

        for cell in range(4):
            values = features[:, cell, window, :].reshape(wide, local)
            hidden = applied(first_net, values)
            hidden = jnp.concatenate(
                [hidden[SUB * o : SUB * (o + 1)] + bias_in[o] for o in range(16)], axis=0
            )
            hidden = hidden / (1.0 + jnp.exp(-hidden))
            terms = applied(second_net, hidden)
            totals[:, cell, window, :] += terms.reshape(2, 3 * SUB, local)

    def section_step(index, carry):
        chunk = lax.rem(index, chunks)
        first = index < chunks
        keep = jnp.where(first, 0.0, 0.75).astype(jnp.float32)
        blend = jnp.where(first, 1.0, 0.25).astype(jnp.float32)
        finish(chunk, index, keep, blend)

        slopes(now, chunk, index + chunks)
        send(index + chunks)
        gather_local(chunk, index + chunks)

        @pl.when(index == 1)
        def _():
            clear_columns()

        @pl.when(index == chunks)
        def _():
            build_nets()

        return carry

    lax.fori_loop(0, 2 * chunks, section_step, 0)

    column_copy = pltpu.make_async_remote_copy(
        src_ref=features.at[:, :, pl.ds(pl.multiple_of(GUARD + place(0), SUB), SUB), :],
        dst_ref=features.at[
            :, :, pl.ds(pl.multiple_of(jnp.where(lev == 0, GUARD - SUB, GUARD + levels), SUB), SUB), :
        ],
        send_sem=col_send_sem,
        recv_sem=col_recv_sem,
        device_id={"lev": 1 - lev},
        device_id_type=MESH,
    )

    def last_step(index, carry):
        chunk = index - 2 * chunks
        finish(chunk, index, jnp.float32(1.0 / 3.0), jnp.float32(2.0 / 3.0))
        at = pl.ds(place(chunk), SUB)
        column = pl.ds(pl.multiple_of(GUARD + place(chunk), SUB), SUB)
        for cell in range(4):
            for tracer in range(2):
                features[tracer, cell, column, :] = cell_inv[cell] * sum(
                    mass[pl.ds(node, 1), :] * now[node, tracer, at, :] for node in cells[cell]
                )
                features[2 + tracer, cell, column, :] = -cell_inv[cell] * sum(
                    wind[node, tracer, at, :] for node in cells[cell]
                )
        for node in range(16):
            for tracer in range(2):
                next_out[node, tracer, at, :] = now[node, tracer, at, :]

        @pl.when(chunk == 0)
        def _():
            column_copy.start()

        @pl.when(chunk == 1)
        def _():
            column_copy.wait()
            column_net(jnp.where(lev == 0, GUARD + levels, GUARD - SUB))

        @pl.when(chunk >= 1)
        def _():
            column_net(GUARD + place(chunk - 1))

        return carry

    lax.fori_loop(2 * chunks, 3 * chunks, last_step, 0)
    column_net(GUARD + place(chunks - 1))
    for cell in range(4):
        for tracer in range(2):
            sub_out[tracer, cell] = totals[tracer, cell, pl.ds(GUARD, levels), :]

    def drain(index, carry):
        edge_copy(0, index).wait_send()
        edge_copy(1, index).wait_send()
        return carry

    lax.fori_loop(0, 3 * chunks, drain, 0)

    for side in range(2):
        mass_copies[side].wait_send()


def per_device(
    tracer_field, velocity, node_mass, neighbours, seam_flips, conv_in, bias_in, conv_out, bias_out
):
    devices = lax.axis_size("elem")
    tracers, levels, nodes, local = tracer_field.shape
    steps = 3 * (levels // SUB)
    f32 = jnp.float32
    vmem = pl.BlockSpec(memory_space=pltpu.VMEM)
    smem = pl.BlockSpec(memory_space=pltpu.SMEM)
    hbm = pl.BlockSpec(memory_space=pl.ANY)
    tall = levels + 2 * GUARD
    by_node, by_cell = pl.pallas_call(
        functools.partial(kernel, devices),
        out_shape=(
            jax.ShapeDtypeStruct((nodes, tracers, levels, local), f32),
            jax.ShapeDtypeStruct((tracers, 4, levels, local), f32),
        ),
        in_specs=[hbm, hbm, vmem, vmem, vmem, smem, smem, smem, smem],
        out_specs=(vmem, vmem),
        scratch_shapes=[
            pltpu.VMEM((nodes, tracers, levels, local), f32),
            pltpu.VMEM((nodes, tracers, levels, local), f32),
            pltpu.VMEM((nodes, 2, levels, local), f32),
            pltpu.VMEM((steps, nodes, tracers, SUB, local), f32),
            pltpu.VMEM((steps // 3, nodes, tracers, SUB, local), f32),
            pltpu.VMEM((2, steps, 4, tracers, SUB, local), f32),
            pltpu.VMEM((nodes, SUB, local), f32),
            pltpu.VMEM((4, SUB, local), f32),
            pltpu.VMEM((6, local, local), jnp.bfloat16),
            pltpu.VMEM((2, 8, local), f32),
            pltpu.VMEM((4, 4, tall, local), f32),
            pltpu.VMEM((2, 4, tall, local), f32),
            pltpu.VMEM((2 * 16 * SUB, 2 * 4 * 3 * SUB), jnp.bfloat16),
            pltpu.VMEM((2 * 2 * 3 * SUB, 2 * 16 * SUB), jnp.bfloat16),
            pltpu.SemaphoreType.DMA((levels // SUB, 2, nodes)),
            pltpu.SemaphoreType.DMA((2, steps)),
            pltpu.SemaphoreType.DMA((2, steps)),
            pltpu.SemaphoreType.DMA((2,)),
            pltpu.SemaphoreType.DMA((2,)),
            pltpu.SemaphoreType.DMA,
            pltpu.SemaphoreType.DMA,
        ],
        compiler_params=pltpu.CompilerParams(
            collective_id=0, has_side_effects=True, vmem_limit_bytes=60 * 2**20
        ),
    )(
        tracer_field, velocity, node_mass, neighbours, seam_flips,
        jnp.transpose(conv_in, (0, 2, 1)), bias_in, conv_out, bias_out,
    )
    return jnp.transpose(by_node, (1, 2, 0, 3)), jnp.transpose(by_cell, (0, 2, 1, 3))


def solution(mesh):
    return jax.shard_map(
        per_device,
        mesh=mesh,
        in_specs=(
            P(None, "lev", None, ("grp", "elem")),
            P(None, "lev", None, ("grp", "elem")),
            P(None, ("grp", "elem")),
            P(None, ("grp", "elem")),
            P(None, ("grp", "elem")),
            P(),
            P(),
            P(),
            P(),
        ),
        out_specs=(P(None, "lev", None, ("grp", "elem")), P(None, "lev", None, ("grp", "elem"))),
        check_vma=False,
    )
```
